512 devices in a mesh: blk: 32 (over z, y_lo), roll: 16 (over x, y_hi, core).
Axes of the slice: x: 4, y: 4 (y_hi: 2, y_lo: 2; y = y_hi * 2 + y_lo), z: 16, core: 2. Of those that a mesh axis runs over, the one named last changes fastest.
Arguments:
- p_query: bfloat16 [512, 4096], P('roll', 'blk'), may hold values from -6 to 6
- p_key: bfloat16 [512, 512], P(('blk', 'roll')), may hold values from -6 to 6
- p_value: bfloat16 [512, 512], P(('blk', 'roll')), may hold values from -6 to 6
- p_out: bfloat16 [512, 4096], P('roll', 'blk'), may hold values from -6 to 6
- p_grad: bfloat16 [512, 4096], P('roll', 'blk'), may hold values from -3 to 3
- p_lse: float32 [512, 32], P('roll', 'blk')
- r_query: bfloat16 [16, 3072, 4096], P('roll', 'blk'), may hold values from -6 to 6
- r_key: bfloat16 [16, 3072, 512], P('roll', 'blk'), may hold values from -6 to 6
- r_value: bfloat16 [16, 3072, 512], P('roll', 'blk'), may hold values from -6 to 6
- r_out: bfloat16 [16, 3072, 4096], P('roll', 'blk'), may hold values from -6 to 6
- r_grad: bfloat16 [16, 3072, 4096], P('roll', 'blk'), may hold values from -3 to 3
- r_lse: float32 [16, 3072, 32], P('roll', 'blk')
- lengths: int32 [16], P('roll'), may hold values from 1024 to 3072, as said below
Outputs:
- p_dq: bfloat16 [512, 4096], P('roll', 'blk')
- p_dk: bfloat16 [512, 512], P(('blk', 'roll'))
- p_dv: bfloat16 [512, 512], P(('blk', 'roll'))
- r_dq: bfloat16 [16, 3072, 4096], P('roll', 'blk')
- r_dk: bfloat16 [16, 3072, 512], P('roll', 'blk')
- r_dv: bfloat16 [16, 3072, 512], P('roll', 'blk')
The draws below stay inside these ranges and needn't reach their ends.
Inputs may be any that keep to these rules, and one draw needn't show every extreme that they name: `lengths`: each length is a multiple of 16 and some rollout fills all 3072 positions.
All inputs are finite; a program needn't handle non-finite values.
Results may differ from the reference program's by a relative error of at most 0.018.
Values may be sent and summed in bfloat16 or wider, within the bound.
No kernel may reach another device: no remote copies, remote signals or barrier semaphores. Data moves between devices by JAX's collectives and lax.ppermute only.
A program may use at most 64 MiB of HBM per device.

```python
import jax
import jax.numpy as jnp
from jax import lax

HQ = 32
KVH = 4
HD = 128
GRP = 8
PROMPT = 512
SLOTS = 3072
NR = 16
N_BLK = 32


def lse_noise(key, shape, spread):
    return jax.random.uniform(key, shape, jnp.float32, -spread, spread)


def draw_p_lse(key, part):
    key = jax.random.fold_in(key, 11)
    counts = jnp.arange(PROMPT, dtype=jnp.float32) + 1.0
    noise = lse_noise(key, (PROMPT, HQ), 0.25)
    return jnp.log(counts)[:, None] + 0.5 + noise


def draw_r_lse(key, part):
    key = jax.random.fold_in(key, 12)
    counts = jnp.arange(SLOTS, dtype=jnp.float32) + 1.0 + PROMPT
    noise = lse_noise(key, (NR, SLOTS, HQ), 0.25)
    return jnp.log(counts)[None, :, None] + 0.5 + noise


def draw_lengths(key, part):
    key = jax.random.fold_in(key, 13)
    first_key, second_key = jax.random.split(key)
    base = jax.random.randint(first_key, (NR,), SLOTS // 48, SLOTS // 16 + 1) * 16
    chosen = jax.random.randint(second_key, (), 0, NR)
    return jnp.where(jnp.arange(NR) == chosen, SLOTS, base).astype(jnp.int32)


def level_of(stream_key, extent, pieces, least, high):
    factor_of, own = 1.0, jax.random.fold_in(stream_key, 6)
    for axis_at, shards_of in pieces:
        steps = jnp.exp(jax.random.uniform(jax.random.fold_in(own, axis_at), (shards_of,), jnp.float32, least / len(pieces), high / len(pieces)))
        factor_of = factor_of * jnp.repeat(steps, extent[axis_at] // shards_of).reshape([-1 if axis == axis_at else 1 for axis in range(len(extent))])
    return factor_of


def normal_values(key, shape, scale, bound, cuts=(), held_as=jnp.bfloat16):
    drawn = scale * jax.random.normal(key, shape, jnp.float32)
    if cuts:
        drawn = drawn * level_of(key, shape, cuts, -0.22, 0.18)
    return jnp.clip(drawn, -bound, bound).astype(held_as)


def setup_inputs(seed: int = 0) -> dict:
    key_list = jax.random.split(jax.random.key(seed), 14)
    return {
        "p_query": normal_values(key_list[0], (PROMPT, HQ * HD), 1.0, 6.0, ((0, 16), (1, 32))),
        "p_key": normal_values(key_list[1], (PROMPT, KVH * HD), 1.0, 6.0, ((0, 512),)),
        "p_value": normal_values(key_list[2], (PROMPT, KVH * HD), 1.0, 6.0, ((0, 512),)),
        "p_out": normal_values(key_list[3], (PROMPT, HQ * HD), 1.0, 6.0, ((0, 16), (1, 32))),
        "p_grad": normal_values(key_list[4], (PROMPT, HQ * HD), 0.5, 3.0, ((0, 16), (1, 32))),
        "p_lse": draw_p_lse(jax.random.fold_in(key_list[13], 71), 0),
        "r_query": normal_values(key_list[6], (NR, SLOTS, HQ * HD), 1.0, 6.0, ((0, 16), (1, 32))),
        "r_key": normal_values(key_list[7], (NR, SLOTS, KVH * HD), 1.0, 6.0, ((0, 16), (1, 32))),
        "r_value": normal_values(key_list[8], (NR, SLOTS, KVH * HD), 1.0, 6.0, ((0, 16), (1, 32))),
        "r_out": normal_values(key_list[9], (NR, SLOTS, HQ * HD), 1.0, 6.0, ((0, 16), (1, 32))),
        "r_grad": normal_values(key_list[10], (NR, SLOTS, HQ * HD), 0.5, 3.0, ((0, 16), (1, 32))),
        "r_lse": draw_r_lse(jax.random.fold_in(key_list[13], 71), 0),
        "lengths": draw_lengths(jax.random.fold_in(key_list[13], 71), 0),
    }


def head_backward(query, grads, lse_rows, delta_rows, keys, values, allowed, parts):
    scale = HD ** -0.5
    high = lax.Precision.HIGHEST
    scores = jnp.einsum("rqd,cd->qrc", query, keys, precision=high) * scale
    probs = jnp.where(allowed[None], jnp.exp(scores - lse_rows.T[:, :, None]), 0.0)
    dprobs = jnp.einsum("rqd,cd->qrc", grads, values, precision=high)
    dscores = lax.optimization_barrier((probs * (dprobs - delta_rows.T[:, :, None])).astype(jnp.bfloat16)).astype(jnp.float32)
    weights = lax.optimization_barrier(probs.astype(jnp.bfloat16)).astype(jnp.float32)
    dquery = jnp.einsum("qrc,cd->rqd", dscores, keys, precision=high) * scale
    height = query.shape[0]
    count = keys.shape[0]
    heads = query.shape[1]
    split_scores = dscores.reshape(heads, parts, height // parts, count)
    split_weights = weights.reshape(heads, parts, height // parts, count)
    blocked_query = query.reshape(parts, height // parts, heads, HD)
    blocked_grads = grads.reshape(parts, height // parts, heads, HD)
    dkeys = jnp.einsum("qbrc,brqd->bcd", split_scores, blocked_query, precision=high) * scale
    dvalues = jnp.einsum("qbrc,brqd->bcd", split_weights, blocked_grads, precision=high)
    return dquery, dkeys, dvalues


def attend(query, grads, lse_rows, delta_rows, keys, values, allowed, parts):
    height = query.shape[0]
    count = keys.shape[0]
    q_heads = query.astype(jnp.float32).reshape(height, KVH, GRP, HD).transpose(1, 0, 2, 3)
    g_heads = grads.astype(jnp.float32).reshape(height, KVH, GRP, HD).transpose(1, 0, 2, 3)
    lse_heads = lse_rows.reshape(height, KVH, GRP).transpose(1, 0, 2)
    delta_heads = delta_rows.reshape(height, KVH, GRP).transpose(1, 0, 2)
    k_heads = keys.astype(jnp.float32).reshape(count, KVH, HD).transpose(1, 0, 2)
    v_heads = values.astype(jnp.float32).reshape(count, KVH, HD).transpose(1, 0, 2)

    def one_head(items):
        return head_backward(items[0], items[1], items[2], items[3], items[4], items[5], allowed, parts)

    dquery, dkeys, dvalues = lax.map(one_head, (q_heads, g_heads, lse_heads, delta_heads, k_heads, v_heads))
    dquery = dquery.transpose(1, 0, 2, 3).reshape(height, HQ * HD)
    dkeys = dkeys.transpose(1, 2, 0, 3).reshape(parts, count, KVH * HD)
    dvalues = dvalues.transpose(1, 2, 0, 3).reshape(parts, count, KVH * HD)
    return dquery, dkeys, dvalues


def row_delta(grads, outputs):
    count = grads.shape[0]
    return jnp.sum(grads.astype(jnp.float32).reshape(count, HQ, HD) * outputs.astype(jnp.float32).reshape(count, HQ, HD), axis=2)


def reference(p_query, p_key, p_value, p_out, p_grad, p_lse, r_query, r_key, r_value, r_out, r_grad, r_lse, lengths):
    positions = jnp.arange(PROMPT)
    prompt_mask = positions[:, None] >= positions[None, :]
    p_dq, p_dk_parts, p_dv_parts = attend(p_query, p_grad, p_lse, row_delta(p_grad, p_out), p_key, p_value, prompt_mask, 1)
    slots = jnp.arange(SLOTS)

    def round_add(totals, terms):
        first = (totals[0].astype(jnp.float32) + terms[0]).astype(jnp.bfloat16)
        second = (totals[1].astype(jnp.float32) + terms[1]).astype(jnp.bfloat16)
        return (first, second), None

    def one_rollout(carry, items):
        query, key, value, output, grad, lse, length = items
        live = slots < length
        allowed = jnp.concatenate([jnp.broadcast_to(live[:, None], (SLOTS, PROMPT)), live[:, None] & (slots[:, None] >= slots[None, :])], axis=1)
        keys = jnp.concatenate([p_key, key], axis=0)
        values = jnp.concatenate([p_value, value], axis=0)
        dquery, dkeys, dvalues = attend(query, grad, lse, row_delta(grad, output), keys, values, allowed, N_BLK)
        carry = (carry[0] + jnp.sum(dkeys[:, :PROMPT], axis=0), carry[1] + jnp.sum(dvalues[:, :PROMPT], axis=0))
        start = (jnp.zeros((SLOTS, KVH * HD), jnp.bfloat16), jnp.zeros((SLOTS, KVH * HD), jnp.bfloat16))
        sums, _ = lax.scan(round_add, start, (dkeys[:, PROMPT:], dvalues[:, PROMPT:]))
        return carry, (dquery.astype(jnp.bfloat16), sums[0], sums[1])

    sums, results = lax.scan(one_rollout, (p_dk_parts[0], p_dv_parts[0]), (r_query, r_key, r_value, r_out, r_grad, r_lse, lengths))
    return p_dq.astype(jnp.bfloat16), sums[0].astype(jnp.bfloat16), sums[1].astype(jnp.bfloat16), results[0], results[1], results[2]
```

```python
import functools

import jax
import jax.numpy as jnp
from jax import lax
from jax.experimental import pallas as pl
from jax.experimental.pallas import tpu as pltpu
from jax.sharding import PartitionSpec as P

KVH = 4
HD = 128
GRP = 8
SCALE = HD ** (-0.5)
LOG2E = 1.4426950408889634
DEAD = 1e30

F32 = jnp.float32
BF16 = jnp.bfloat16
NN = (((1,), (0,)), ((), ()))
NT = (((1,), (1,)), ((), ()))
TN = (((0,), (0,)), ((), ()))


def dot(left, right, dims):
    return lax.dot_general(left, right, dims, preferred_element_type=F32)


def weigh(keys, values, query, grads, lse_row, delta_row, keep):
    scores = dot(keys, query, NT)
    dprobs = dot(values, grads, NT)
    probs = jnp.exp2(scores * (SCALE * LOG2E) - lse_row)
    if keep is not None:
        probs = jnp.where(keep, probs, 0.0)
    dscores = (probs * (dprobs - delta_row)).astype(BF16)
    return probs.astype(BF16), dscores


def kernel(
    info, q_ref, g_ref, rows_ref, pq_ref, pg_ref, prows_ref, kv_ref,
    dq_ref, dkv_ref, pdq_ref,
    qs, gs, wts, dsc, acc, pkv,
    *, span, share,
):
    square, live, first = info[0], info[1], info[2]
    pitch = span + share
    squares = kv_ref.shape[0] // pitch
    plen = squares * share
    for h in range(GRP):
        qs[h * span : (h + 1) * span, :] = q_ref[:, h * HD : (h + 1) * HD]
        gs[h * span : (h + 1) * span, :] = g_ref[:, h * HD : (h + 1) * HD]
    acc[...] = jnp.zeros_like(acc)

    def heads(keys, values, count, keep):
        for h in range(GRP):
            at = slice(h * span, (h + 1) * span)
            weights, dscores = weigh(
                keys, values, qs[at, :], gs[at, :],
                rows_ref[h : h + 1, :], rows_ref[GRP + h : GRP + h + 1, :], keep,
            )
            wts[0:count, at] = weights
            dsc[0:count, at] = dscores
            acc[at, :] += dot(dscores, keys, TN)
        dkeys = dot(dsc[0:count, :], qs[...], NN) * SCALE
        dvalues = dot(wts[0:count, :], gs[...], NN)
        return dkeys, dvalues

    for j in range(squares):
        pkv[j * share : (j + 1) * share, :] = kv_ref[j * pitch + span : (j + 1) * pitch, :]

    keys, values = pkv[:, 0:HD], pkv[:, HD : 2 * HD]
    spot = lax.broadcasted_iota(jnp.int32, (plen, pq_ref.shape[0]), 0)
    row = lax.broadcasted_iota(jnp.int32, (plen, pq_ref.shape[0]), 1) + first
    weights, dscores = weigh(
        keys, values, pq_ref[...], pg_ref[...], prows_ref[0:1, :], prows_ref[1:2, :], spot <= row
    )
    pdq_ref[...] = (dot(dscores, keys, TN) * SCALE).astype(BF16)
    own_dk = dot(dscores, pq_ref[...], NN) * SCALE
    own_dv = dot(weights, pg_ref[...], NN)

    def put_prompt(dkeys, dvalues):
        for j in range(squares):
            at = slice(j * share, (j + 1) * share)
            to = slice(j * pitch + span, (j + 1) * pitch)
            dkv_ref[to, 0:HD] = dkeys[at, :].astype(BF16)
            dkv_ref[to, HD : 2 * HD] = dvalues[at, :].astype(BF16)

    def put(base, dkeys, dvalues):
        dkv_ref[pl.ds(base, span), 0:HD] = dkeys.astype(BF16)
        dkv_ref[pl.ds(base, span), HD : 2 * HD] = dvalues.astype(BF16)

    def empty(j, carry):
        dkv_ref[pl.ds(pl.multiple_of(j * pitch, 16), span), :] = jnp.zeros((span, 2 * HD), BF16)
        return carry

    @pl.when(live == 0)
    def _():
        put_prompt(own_dk, own_dv)
        lax.fori_loop(0, squares, empty, 0)

    @pl.when(live != 0)
    def _():
        dkeys, dvalues = heads(keys, values, plen, None)
        put_prompt(own_dk + dkeys, own_dv + dvalues)

        def whole(j, carry):
            base = pl.multiple_of(j * pitch, 16)
            tile = kv_ref[pl.ds(base, span), :]
            put(base, *heads(tile[:, 0:HD], tile[:, HD : 2 * HD], span, None))
            return carry

        lax.fori_loop(0, square, whole, 0)
        base = pl.multiple_of(square * pitch, 16)
        tile = kv_ref[pl.ds(base, span), :]
        spot = lax.broadcasted_iota(jnp.int32, (span, span), 0)
        row = lax.broadcasted_iota(jnp.int32, (span, span), 1)
        put(base, *heads(tile[:, 0:HD], tile[:, HD : 2 * HD], span, spot <= row))
        lax.fori_loop(square + 1, squares, empty, 0)

    for h in range(GRP):
        dq_ref[:, h * HD : (h + 1) * HD] = (acc[h * span : (h + 1) * span, :] * SCALE).astype(BF16)


def backward(info, query, grads, rows, p_query, p_grad, p_rows, kv, span, share):
    squares = kv.shape[0] // (span + share)
    plen = squares * share
    widest = max(span, plen)
    pairs = GRP * span * (plen + (squares + 1) * span // 2)
    vmem = pl.BlockSpec(memory_space=pltpu.VMEM)
    return pl.pallas_call(
        functools.partial(kernel, span=span, share=share),
        out_shape=(
            jax.ShapeDtypeStruct(query.shape, BF16),
            jax.ShapeDtypeStruct(kv.shape, BF16),
            jax.ShapeDtypeStruct(p_query.shape, BF16),
        ),
        in_specs=[pl.BlockSpec(memory_space=pltpu.SMEM)] + [vmem] * 7,
        out_specs=(vmem, vmem, vmem),
        scratch_shapes=[
            pltpu.VMEM((GRP * span, HD), BF16),
            pltpu.VMEM((GRP * span, HD), BF16),
            pltpu.VMEM((widest, GRP * span), BF16),
            pltpu.VMEM((widest, GRP * span), BF16),
            pltpu.VMEM((GRP * span, HD), F32),
            pltpu.VMEM((plen, 2 * HD), BF16),
        ],
        compiler_params=pltpu.CompilerParams(vmem_limit_bytes=40 * 1024 * 1024),
        cost_estimate=pl.CostEstimate(
            flops=pairs * HD * 10, bytes_accessed=6 * 1024 * 1024, transcendentals=pairs
        ),
    )(info, query, grads, rows, p_query, p_grad, p_rows, kv)


def row_delta(grads, outputs):
    height = grads.shape[0]
    heads = grads.shape[1] // HD
    return jnp.sum(
        grads.reshape(height, heads, HD).astype(F32) * outputs.reshape(height, heads, HD).astype(F32),
        axis=2,
    )


def on_device(
    p_query, p_key, p_value, p_out, p_grad, p_lse,
    r_query, r_key, r_value, r_out, r_grad, r_lse, lengths,
):
    blocks = lax.axis_size("blk")
    rolls = lax.axis_size("roll")
    owner = lax.axis_index("blk")
    member = lax.axis_index("roll")
    squares = blocks // KVH
    square = owner // KVH
    rows = r_query.shape[1]
    span = KVH * rows
    near = [[s * KVH + m for m in range(KVH)] for s in range(squares)]
    far = [[s * KVH + m for s in range(squares)] for m in range(KVH)]
    width = GRP * HD

    def trade(block):
        return lax.all_to_all(block, "blk", 0, 0, tiled=True, axis_index_groups=near)

    own = jnp.concatenate([p_key, p_value], axis=1)
    sent = jnp.broadcast_to(own[None], (rolls,) + own.shape)
    prompt = lax.all_to_all(sent, "roll", 0, 0, tiled=True).reshape(-1, own.shape[1])
    part = prompt.shape[0]
    share = KVH * part

    both = jnp.concatenate([jnp.concatenate([r_key[0], r_value[0]], axis=1), prompt], axis=0)
    height = both.shape[0]
    both = both.reshape(height, 2, KVH, HD).transpose(2, 0, 1, 3).reshape(KVH, height, 2 * HD)
    both = trade(both)
    both = jnp.concatenate(
        [both[:, :rows].reshape(span, 2 * HD), both[:, rows:].reshape(share, 2 * HD)], axis=0
    )
    kv = lax.all_gather(both, "blk", axis=0, tiled=True, axis_index_groups=far)

    def spread(block):
        return trade(block.reshape(rows, KVH, width).transpose(1, 0, 2)).reshape(span, width)

    query = spread(r_query[0])
    grads = spread(r_grad[0])
    position = owner * rows + jnp.arange(rows)
    alive = position < lengths[0]
    lse_rows = jnp.where(alive[:, None], r_lse[0] * LOG2E, DEAD)
    delta = row_delta(r_grad[0], r_out[0])
    pair = jnp.stack([lse_rows.T.reshape(KVH, GRP, rows), delta.T.reshape(KVH, GRP, rows)], axis=1)
    pair = trade(pair.reshape(KVH, 2 * GRP, rows)).transpose(1, 0, 2).reshape(2 * GRP, span)

    there = [(m * squares + s, s * KVH + m) for m in range(KVH) for s in range(squares)]
    back = [(b, a) for a, b in there]
    p_rows = jnp.concatenate([p_lse * LOG2E, row_delta(p_grad, p_out)], axis=1).T
    p_pack = lax.ppermute(jnp.concatenate([p_query, p_grad], axis=1), "blk", there)
    p_rows = lax.ppermute(p_rows, "blk", there)

    info = jnp.stack(
        [square, (square * span < lengths[0]).astype(jnp.int32), member * p_query.shape[0]]
    ).astype(jnp.int32)
    dq, dkv, p_dq = backward(
        info, query, grads, pair, p_pack[:, :HD], p_pack[:, HD:], p_rows, kv, span, share
    )
    p_dq = lax.ppermute(p_dq, "blk", back)
    summed = lax.psum_scatter(dkv, "blk", scatter_dimension=0, tiled=True, axis_index_groups=far)
    r_dq = trade(dq.reshape(KVH, rows, width)).transpose(1, 0, 2).reshape(1, rows, KVH * width)

    summed = jnp.concatenate(
        [
            summed[:span].reshape(KVH, rows, 2 * HD),
            summed[span:].reshape(KVH, part, 2 * HD),
        ],
        axis=1,
    )
    summed = trade(summed).reshape(KVH, height, 2, HD).transpose(2, 1, 0, 3)
    summed = summed.reshape(2, height, KVH * HD)
    terms = summed[:, rows:].reshape(2, rolls, part // rolls, KVH * HD).transpose(1, 0, 2, 3)
    terms = lax.all_to_all(terms, "roll", 0, 0, tiled=True)
    total = jnp.sum(terms.astype(F32), axis=0).astype(BF16)
    return (p_dq, total[0], total[1], r_dq, summed[0, :rows][None], summed[1, :rows][None])


def solution(mesh):
    placed = (
        P("roll", "blk"),
        P(("blk", "roll"), None),
        P(("blk", "roll"), None),
        P("roll", "blk"),
        P("roll", "blk"),
        P("roll", "blk"),
        P("roll", "blk", None),
        P("roll", "blk", None),
        P("roll", "blk", None),
        P("roll", "blk", None),
        P("roll", "blk", None),
        P("roll", "blk", None),
        P("roll"),
    )
    return jax.shard_map(
        on_device,
        mesh=mesh,
        in_specs=placed,
        out_specs=(
            P("roll", "blk"),
            P(("blk", "roll"), None),
            P(("blk", "roll"), None),
            P("roll", "blk", None),
            P("roll", "blk", None),
            P("roll", "blk", None),
        ),
        check_vma=False,
    )
```

```python
import functools

import jax
import jax.numpy as jnp
from jax import lax
from jax.experimental import pallas as pl
from jax.experimental.pallas import tpu as pltpu
from jax.sharding import PartitionSpec as P

KVH = 4
HD = 128
GRP = 8
SCALE = HD ** (-0.5)
LOG2E = 1.4426950408889634
DEAD = 1e30

F32 = jnp.float32
BF16 = jnp.bfloat16
NN = (((1,), (0,)), ((), ()))
NT = (((1,), (1,)), ((), ()))
TN = (((0,), (0,)), ((), ()))


def dot(left, right, dims):
    return lax.dot_general(left, right, dims, preferred_element_type=F32)


def weigh(keys, values, query, grads, lse_row, delta_row, keep):
    scores = dot(keys, query, NT)
    dprobs = dot(values, grads, NT)
    probs = jnp.exp2(scores * (SCALE * LOG2E) - lse_row)
    if keep is not None:
        probs = jnp.where(keep, probs, 0.0)
    dscores = (probs * (dprobs - delta_row)).astype(BF16)
    return probs.astype(BF16), dscores


def terms(refs, keys, values, at, keep, acc):
    q_ref, g_ref, rows_ref = refs
    weights, dscores = weigh(
        keys, values, q_ref[at, :], g_ref[at, :], rows_ref[0:1, at], rows_ref[1:2, at], keep
    )
    acc[:, at] += dot(keys.T, dscores, NN)
    return dot(dscores, q_ref[at, :], NN), dot(weights, g_ref[at, :], NN)


def own_kernel(info, q_ref, g_ref, rows_ref, spot_ref, kv_ref, d_ref, acc):
    live = info[1]
    chunk = kv_ref.shape[0] // KVH
    group = q_ref.shape[0] // KVH
    acc[...] = jnp.zeros_like(acc)
    d_ref[...] = jnp.zeros_like(d_ref)

    @pl.when(live != 0)
    def _():
        for c in range(KVH):
            reach = (c + 1) * chunk
            place = lax.broadcasted_iota(jnp.int32, (reach, group), 0)
            dk, dv = terms(
                (q_ref, g_ref, rows_ref), kv_ref[0:reach, 0:HD], kv_ref[0:reach, HD : 2 * HD],
                slice(c * group, (c + 1) * group), place <= spot_ref[...] + c * chunk, acc,
            )
            d_ref[0:reach, 0:HD] += dk * SCALE
            d_ref[0:reach, HD : 2 * HD] += dv


def lower_kernel(info, q_ref, g_ref, rows_ref, kv_ref, dq_in, d_ref, dq_ref, acc, *, span):
    square, live = info[0], info[1]
    squares = kv_ref.shape[0] // span
    columns = q_ref.shape[0]
    group = columns // KVH
    acc[...] = dq_in[...]
    used = jnp.where(live != 0, square, 0)

    def whole(j, carry):
        block = pl.ds(pl.multiple_of(j * span, 16), span)
        keys, values = kv_ref[block, 0:HD], kv_ref[block, HD : 2 * HD]
        dkeys = dvalues = 0.0
        for c in range(0, columns, 2 * group):
            dk, dv = terms((q_ref, g_ref, rows_ref), keys, values, slice(c, c + 2 * group), None, acc)
            dkeys, dvalues = dkeys + dk, dvalues + dv
        d_ref[block, 0:HD] = (dkeys * SCALE).astype(BF16)
        d_ref[block, HD : 2 * HD] = dvalues.astype(BF16)
        return carry

    def empty(j, carry):
        d_ref[pl.ds(pl.multiple_of(j * span, 16), span), :] = jnp.zeros((span, 2 * HD), BF16)
        return carry

    lax.fori_loop(0, used, whole, 0)
    lax.fori_loop(used, squares, empty, 0)
    dq_ref[...] = (acc[...].T * SCALE).astype(BF16)


def prompt_kernel(
    info, q_ref, g_ref, rows_ref, pq_ref, pg_ref, prows_ref, kv_ref, dq_in,
    d_ref, dq_ref, pdq_ref, acc, total,
    *, blocks,
):
    live, start = info[1], info[2]
    columns = q_ref.shape[0]
    group = columns // KVH
    plen = kv_ref.shape[0]
    rolls = plen // blocks
    acc[...] = dq_in[...]
    keys, values = kv_ref[:, 0:HD], kv_ref[:, HD : 2 * HD]
    shape = (plen, pq_ref.shape[0])
    index = lax.broadcasted_iota(jnp.int32, shape, 0)
    place = lax.rem(index, blocks) * rolls + lax.div(index, blocks)
    row = lax.broadcasted_iota(jnp.int32, shape, 1) + start
    weights, dscores = weigh(
        keys, values, pq_ref[...], pg_ref[...], prows_ref[0:1, :], prows_ref[1:2, :], place <= row
    )
    pdq_ref[...] = (dot(dscores, keys, TN) * SCALE).astype(BF16)
    total[:, 0:HD] = dot(dscores, pq_ref[...], NN)
    total[:, HD : 2 * HD] = dot(weights, pg_ref[...], NN)

    @pl.when(live != 0)
    def _():
        for c in range(0, columns, 2 * group):
            at = slice(c, c + 2 * group)
            dk, dv = terms((q_ref, g_ref, rows_ref), keys, values, at, None, acc)
            total[:, 0:HD] += dk
            total[:, HD : 2 * HD] += dv

    d_ref[:, 0:HD] = (total[:, 0:HD] * SCALE).astype(BF16)
    d_ref[:, HD : 2 * HD] = total[:, HD : 2 * HD].astype(BF16)
    dq_ref[...] = acc[...]


def call(body, info, operands, outs, scratch, pairs):
    vmem = pl.BlockSpec(memory_space=pltpu.VMEM)
    return pl.pallas_call(
        body,
        out_shape=outs,
        in_specs=[pl.BlockSpec(memory_space=pltpu.SMEM)] + [vmem] * len(operands),
        out_specs=(vmem,) * len(outs),
        scratch_shapes=scratch,
        compiler_params=pltpu.CompilerParams(vmem_limit_bytes=40 * 1024 * 1024),
        cost_estimate=pl.CostEstimate(
            flops=pairs * HD * 10, bytes_accessed=4 * 1024 * 1024, transcendentals=pairs
        ),
    )(info, *operands)


def own_backward(info, fixed, spot, block):
    turned = fixed[0].shape[::-1]
    return call(
        own_kernel,
        info,
        (*fixed, spot, block),
        (jax.ShapeDtypeStruct(block.shape, F32), jax.ShapeDtypeStruct(turned, F32)),
        [],
        turned[1] * block.shape[0] * 5 // 8,
    )


def lower_backward(info, fixed, kv, carried, span):
    turned = carried.shape
    return call(
        functools.partial(lower_kernel, span=span),
        info,
        (*fixed, kv, carried),
        (jax.ShapeDtypeStruct(kv.shape, BF16), jax.ShapeDtypeStruct(turned[::-1], BF16)),
        [pltpu.VMEM(turned, F32)],
        turned[1] * kv.shape[0],
    )


def prompt_backward(info, fixed, prompt_rows, kv, carried, blocks):
    turned = carried.shape
    return call(
        functools.partial(prompt_kernel, blocks=blocks),
        info,
        (*fixed, *prompt_rows, kv, carried),
        (
            jax.ShapeDtypeStruct(kv.shape, BF16),
            jax.ShapeDtypeStruct(turned, F32),
            jax.ShapeDtypeStruct(prompt_rows[0].shape, BF16),
        ),
        [pltpu.VMEM(turned, F32), pltpu.VMEM(kv.shape, F32)],
        turned[1] * kv.shape[0],
    )


def row_delta(grads, outputs):
    height = grads.shape[0]
    heads = grads.shape[1] // HD
    return jnp.sum(
        grads.reshape(height, heads, HD).astype(F32) * outputs.reshape(height, heads, HD).astype(F32),
        axis=2,
    )


def on_device(
    p_query, p_key, p_value, p_out, p_grad, p_lse,
    r_query, r_key, r_value, r_out, r_grad, r_lse, lengths,
):
    blocks = lax.axis_size("blk")
    rolls = lax.axis_size("roll")
    owner = lax.axis_index("blk")
    member = lax.axis_index("roll")
    squares = blocks // KVH
    square = owner // KVH
    rows = r_query.shape[1]
    span = KVH * rows
    near = [[s * KVH + m for m in range(KVH)] for s in range(squares)]

    far = [[s * KVH + m for s in range(squares)] for m in range(KVH)]
    part = p_key.shape[0]

    def trade(block):
        return lax.all_to_all(block, "blk", 0, 0, tiled=True, axis_index_groups=near)

    def together(*arrays):
        return lax.optimization_barrier(arrays)

    both = jnp.concatenate(
        [jnp.concatenate([r_key[0], r_value[0]], axis=1), jnp.concatenate([p_key, p_value], axis=1)]
    )
    height = rows + part
    both = both.reshape(height, 2, KVH, HD).transpose(2, 0, 1, 3).reshape(KVH, height, 2 * HD)
    both = trade(both)
    mine = both[:, :rows].reshape(span, 2 * HD)
    prompt = both[:, rows:].reshape(KVH * part, 2 * HD)

    kv = lax.all_gather(mine, "blk", axis=0, tiled=True, axis_index_groups=far)
    r_query, r_grad, r_lse, prompt, mine = together(r_query, r_grad, r_lse, prompt, mine)

    def heads_first(block):
        heads = block.reshape(rows, KVH, GRP, HD).transpose(1, 2, 0, 3)
        return heads.reshape(KVH, GRP * rows, HD)

    query = trade(heads_first(r_query[0])).reshape(KVH * GRP * rows, HD)
    grads = trade(heads_first(r_grad[0])).reshape(KVH * GRP * rows, HD)
    position = owner * rows + jnp.arange(rows)
    alive = position < lengths[0]
    lse_rows = jnp.where(alive[:, None], r_lse[0] * LOG2E, DEAD)
    delta = row_delta(r_grad[0], r_out[0])
    pair = jnp.stack([lse_rows.T.reshape(KVH, GRP, rows), delta.T.reshape(KVH, GRP, rows)], axis=1)
    pair = trade(pair.reshape(KVH, 2 * GRP, rows)).reshape(KVH, 2, GRP * rows)
    pair = pair.transpose(1, 0, 2).reshape(2, KVH * GRP * rows)

    prompt = jnp.broadcast_to(prompt[None], (squares,) + prompt.shape)
    prompt = lax.all_to_all(prompt, "blk", 0, 0, tiled=True, axis_index_groups=far)
    prompt = prompt.reshape(blocks * part, 2 * HD)
    prompt = jnp.broadcast_to(prompt[None], (rolls,) + prompt.shape)
    prompt = lax.all_to_all(prompt, "roll", 0, 0, tiled=True).reshape(-1, 2 * HD)
    prompt = prompt.reshape(rolls, blocks, part, 2 * HD).transpose(0, 2, 1, 3).reshape(-1, 2 * HD)

    there = [(m * squares + s, s * KVH + m) for m in range(KVH) for s in range(squares)]
    back = [(b, a) for a, b in there]
    p_rows = jnp.concatenate([p_lse * LOG2E, row_delta(p_grad, p_out)], axis=1).T
    p_pack = lax.ppermute(jnp.concatenate([p_query, p_grad], axis=1), "blk", there)
    p_rows = lax.ppermute(p_rows, "blk", there)
    prompt_rows = (p_pack[:, :HD], p_pack[:, HD:], p_rows)

    info = jnp.stack(
        [square, square * span < lengths[0], member * p_query.shape[0], squares]
    ).astype(jnp.int32)
    spot = jnp.tile(jnp.arange(rows, dtype=jnp.int32), GRP)[None]
    fixed = (query, grads, pair)

    own, dq = own_backward(info, fixed, spot, mine)
    prompt_terms, dq, p_dq = prompt_backward(info, fixed, prompt_rows, prompt, dq, blocks)
    lower, dq = lower_backward(info, fixed, kv, dq, span)
    lower = lax.psum_scatter(lower, "blk", scatter_dimension=0, tiled=True, axis_index_groups=far)
    summed = (own + lower.astype(F32)).astype(BF16)

    prompt_terms = prompt_terms.reshape(rolls, part, blocks, 2 * HD).transpose(0, 2, 1, 3)
    prompt_terms = lax.all_to_all(prompt_terms.reshape(rolls, blocks * part, 2 * HD), "roll", 0, 0, tiled=True)
    prompt_terms = jnp.sum(prompt_terms.astype(F32), axis=0).astype(BF16)
    prompt_terms = lax.all_to_all(
        prompt_terms.reshape(squares, KVH * part, 2 * HD), "blk", 0, 0, tiled=True, axis_index_groups=far
    )
    prompt_terms = jnp.sum(prompt_terms.astype(F32), axis=0).astype(BF16)

    p_dq = lax.ppermute(p_dq, "blk", back)
    r_dq = trade(dq.reshape(KVH, GRP * rows, HD)).reshape(KVH, GRP, rows, HD)
    summed, r_dq, p_dq = together(summed, r_dq, p_dq)
    r_dq = r_dq.transpose(2, 0, 1, 3).reshape(1, rows, KVH * GRP * HD)

    summed = jnp.concatenate(
        [summed.reshape(KVH, rows, 2 * HD), prompt_terms.reshape(KVH, part, 2 * HD)], axis=1
    )
    summed = trade(summed).reshape(KVH, height, 2, HD).transpose(2, 1, 0, 3)
    summed = summed.reshape(2, height, KVH * HD)
    return (
        p_dq, summed[0, rows:], summed[1, rows:],
        r_dq, summed[0, :rows][None], summed[1, :rows][None],
    )


def solution(mesh):
    placed = (
        P("roll", "blk"),
        P(("blk", "roll"), None),
        P(("blk", "roll"), None),
        P("roll", "blk"),
        P("roll", "blk"),
        P("roll", "blk"),
        P("roll", "blk", None),
        P("roll", "blk", None),
        P("roll", "blk", None),
        P("roll", "blk", None),
        P("roll", "blk", None),
        P("roll", "blk", None),
        P("roll"),
    )
    return jax.shard_map(
        on_device,
        mesh=mesh,
        in_specs=placed,
        out_specs=(
            P("roll", "blk"),
            P(("blk", "roll"), None),
            P(("blk", "roll"), None),
            P("roll", "blk", None),
            P("roll", "blk", None),
            P("roll", "blk", None),
        ),
        check_vma=False,
    )
```

```python
import functools

import jax
import jax.numpy as jnp
from jax import lax
from jax.experimental import pallas as pl
from jax.experimental.pallas import tpu as pltpu
from jax.sharding import PartitionSpec as P

KVH = 4
HD = 128
GRP = 8
SCALE = HD ** (-0.5)
LOG2E = 1.4426950408889634
DEAD = 1e30

F32 = jnp.float32
BF16 = jnp.bfloat16
NN = (((1,), (0,)), ((), ()))
NT = (((1,), (1,)), ((), ()))
TN = (((0,), (0,)), ((), ()))


def dot(left, right, dims):
    return lax.dot_general(left, right, dims, preferred_element_type=F32)


def weigh(keys, values, query, grads, lse_row, delta_row, keep):
    scores = dot(keys, query, NT)
    dprobs = dot(values, grads, NT)
    probs = jnp.exp2(scores * (SCALE * LOG2E) - lse_row)
    if keep is not None:
        probs = jnp.where(keep, probs, 0.0)
    dscores = (probs * (dprobs - delta_row)).astype(BF16)
    return probs.astype(BF16), dscores


def terms(refs, keys, values, at, keep, acc):
    q_ref, g_ref, rows_ref = refs
    weights, dscores = weigh(
        keys, values, q_ref[at, :], g_ref[at, :], rows_ref[0:1, at], rows_ref[1:2, at], keep
    )
    acc[:, at] += dot(keys.T, dscores, NN)
    return dot(dscores, q_ref[at, :], NN), dot(weights, g_ref[at, :], NN)


def own_kernel(info, q_ref, g_ref, rows_ref, spot_ref, kv_ref, d_ref, acc):
    live = info[1]
    chunk = kv_ref.shape[0] // KVH
    group = q_ref.shape[0] // KVH
    acc[...] = jnp.zeros_like(acc)
    d_ref[...] = jnp.zeros_like(d_ref)

    @pl.when(live != 0)
    def _():
        for c in range(KVH):
            reach = (c + 1) * chunk
            place = lax.broadcasted_iota(jnp.int32, (reach, group), 0)
            dk, dv = terms(
                (q_ref, g_ref, rows_ref), kv_ref[0:reach, 0:HD], kv_ref[0:reach, HD : 2 * HD],
                slice(c * group, (c + 1) * group), place <= spot_ref[...] + c * chunk, acc,
            )
            d_ref[0:reach, 0:HD] += dk * SCALE
            d_ref[0:reach, HD : 2 * HD] += dv


def lower_kernel(info, q_ref, g_ref, rows_ref, kv_ref, dq_in, d_ref, acc, *, span, pitch):
    square, live = info[0], info[1]
    squares = kv_ref.shape[0] // pitch
    columns = q_ref.shape[0]
    group = columns // KVH
    acc[...] = dq_in[...]
    used = jnp.where(live != 0, square, 0)

    def whole(j, carry):
        source = pl.ds(pl.multiple_of(j * pitch, 16), span)
        block = pl.ds(pl.multiple_of(j * span, 16), span)
        keys, values = kv_ref[source, 0:HD], kv_ref[source, HD : 2 * HD]
        dkeys = dvalues = 0.0
        for c in range(0, columns, 2 * group):
            dk, dv = terms((q_ref, g_ref, rows_ref), keys, values, slice(c, c + 2 * group), None, acc)
            dkeys, dvalues = dkeys + dk, dvalues + dv
        d_ref[block, 0:HD] = (dkeys * SCALE).astype(BF16)
        d_ref[block, HD : 2 * HD] = dvalues.astype(BF16)
        return carry

    def empty(j, carry):
        d_ref[pl.ds(pl.multiple_of(j * span, 16), span), :] = jnp.zeros((span, 2 * HD), BF16)
        return carry

    lax.fori_loop(0, used, whole, 0)
    lax.fori_loop(used, squares, empty, 0)


def prompt_kernel(
    info, q_ref, g_ref, rows_ref, pq_ref, pg_ref, prows_ref, kv_ref, dq_in,
    d_ref, dq_ref, pdq_ref, acc, total,
    *, blocks,
):
    live, start = info[1], info[2]
    columns = q_ref.shape[0]
    group = columns // KVH
    plen = kv_ref.shape[0]
    rolls = plen // blocks
    acc[...] = dq_in[...]
    keys, values = kv_ref[:, 0:HD], kv_ref[:, HD : 2 * HD]
    shape = (plen, pq_ref.shape[0])
    index = lax.broadcasted_iota(jnp.int32, shape, 0)
    place = lax.rem(index, blocks) * rolls + lax.div(index, blocks)
    row = lax.broadcasted_iota(jnp.int32, shape, 1) + start
    weights, dscores = weigh(
        keys, values, pq_ref[...], pg_ref[...], prows_ref[0:1, :], prows_ref[1:2, :], place <= row
    )
    pdq_ref[...] = (dot(dscores, keys, TN) * SCALE).astype(BF16)
    total[:, 0:HD] = dot(dscores, pq_ref[...], NN)
    total[:, HD : 2 * HD] = dot(weights, pg_ref[...], NN)

    @pl.when(live != 0)
    def _():
        for c in range(0, columns, 2 * group):
            at = slice(c, c + 2 * group)
            dk, dv = terms((q_ref, g_ref, rows_ref), keys, values, at, None, acc)
            total[:, 0:HD] += dk
            total[:, HD : 2 * HD] += dv

    d_ref[:, 0:HD] = (total[:, 0:HD] * SCALE).astype(BF16)
    d_ref[:, HD : 2 * HD] = total[:, HD : 2 * HD].astype(BF16)
    dq_ref[...] = (acc[...].T * SCALE).astype(BF16)


def call(body, info, operands, outs, scratch, pairs):
    vmem = pl.BlockSpec(memory_space=pltpu.VMEM)
    return pl.pallas_call(
        body,
        out_shape=outs,
        in_specs=[pl.BlockSpec(memory_space=pltpu.SMEM)] + [vmem] * len(operands),
        out_specs=(vmem,) * len(outs),
        scratch_shapes=scratch,
        compiler_params=pltpu.CompilerParams(vmem_limit_bytes=40 * 1024 * 1024),
        cost_estimate=pl.CostEstimate(
            flops=pairs * HD * 10, bytes_accessed=4 * 1024 * 1024, transcendentals=pairs
        ),
    )(info, *operands)


def own_backward(info, fixed, spot, block):
    turned = fixed[0].shape[::-1]
    return call(
        own_kernel,
        info,
        (*fixed, spot, block),
        (jax.ShapeDtypeStruct(block.shape, F32), jax.ShapeDtypeStruct(turned, F32)),
        [],
        block.shape[0],
    )


def lower_backward(info, fixed, kv, carried, span, pitch):
    query = fixed[0]
    return call(
        functools.partial(lower_kernel, span=span, pitch=pitch),
        info,
        (*fixed, kv, carried),
        (
            jax.ShapeDtypeStruct((kv.shape[0] // pitch * span, kv.shape[1]), BF16),
            jax.ShapeDtypeStruct(carried.shape, F32),
        ),
        [],
        query.shape[0] * kv.shape[0],
    )


def prompt_backward(info, fixed, prompt_rows, kv, carried, blocks):
    query = fixed[0]
    return call(
        functools.partial(prompt_kernel, blocks=blocks),
        info,
        (*fixed, *prompt_rows, kv, carried),
        (
            jax.ShapeDtypeStruct(kv.shape, BF16),
            jax.ShapeDtypeStruct(query.shape, BF16),
            jax.ShapeDtypeStruct(prompt_rows[0].shape, BF16),
        ),
        [pltpu.VMEM(carried.shape, F32), pltpu.VMEM(kv.shape, F32)],
        query.shape[0] * kv.shape[0],
    )


def row_delta(grads, outputs):
    height = grads.shape[0]
    heads = grads.shape[1] // HD
    return jnp.sum(
        grads.reshape(height, heads, HD).astype(F32) * outputs.reshape(height, heads, HD).astype(F32),
        axis=2,
    )


def three(rows):
    parts = []
    for _ in range(3):
        part = lax.reduce_precision(rows, 8, 7)
        parts.append(part.astype(BF16))
        rows = rows - part
    return jnp.concatenate(parts, axis=1)


def on_device(
    p_query, p_key, p_value, p_out, p_grad, p_lse,
    r_query, r_key, r_value, r_out, r_grad, r_lse, lengths,
):
    blocks = lax.axis_size("blk")
    rolls = lax.axis_size("roll")
    owner = lax.axis_index("blk")
    member = lax.axis_index("roll")
    squares = blocks // KVH
    square = owner // KVH
    rows = r_query.shape[1]
    span = KVH * rows
    near = [[s * KVH + m for m in range(KVH)] for s in range(squares)]

    far = [[s * KVH + m for s in range(squares)] for m in range(KVH)]
    part = p_key.shape[0]

    def trade(block):
        return lax.all_to_all(block, "blk", 0, 0, tiled=True, axis_index_groups=near)

    def together(*arrays):
        return lax.optimization_barrier(arrays)

    both = jnp.concatenate(
        [jnp.concatenate([r_key[0], r_value[0]], axis=1), jnp.concatenate([p_key, p_value], axis=1)]
    )
    height = rows + part
    both = both.reshape(height, 2, KVH, HD).transpose(2, 0, 1, 3).reshape(KVH, height, 2 * HD)
    both = trade(both)
    mine = both[:, :rows].reshape(span, 2 * HD)
    prompt = both[:, rows:].reshape(KVH * part, 2 * HD)

    few = KVH * part
    spare = jnp.zeros((-few % 16, 2 * HD), BF16)
    pitch = span + few + spare.shape[0]
    kv = jnp.concatenate([mine, prompt, spare], axis=0)
    kv = lax.all_gather(kv, "blk", axis=0, tiled=True, axis_index_groups=far)
    r_query, r_grad, r_lse, mine = together(r_query, r_grad, r_lse, mine)

    def heads_first(block):
        heads = block.reshape(rows, KVH, GRP, HD).transpose(1, 2, 0, 3)
        return heads.reshape(KVH, GRP * rows, HD)

    query = trade(heads_first(r_query[0])).reshape(KVH * GRP * rows, HD)
    position = owner * rows + jnp.arange(rows)
    alive = position < lengths[0]
    lse_rows = jnp.where(alive[:, None], r_lse[0] * LOG2E, DEAD)
    delta = row_delta(r_grad[0], r_out[0])
    pair = jnp.stack([lse_rows.T.reshape(KVH, GRP * rows), delta.T.reshape(KVH, GRP * rows)], axis=1)
    pair = three(pair.reshape(KVH, -1, HD))
    grads = trade(jnp.concatenate([heads_first(r_grad[0]), pair], axis=1))
    pair = grads[:, GRP * rows :].reshape(KVH, 3, 2, GRP * rows).astype(F32)
    pair = ((pair[:, 2] + pair[:, 1]) + pair[:, 0]).transpose(1, 0, 2).reshape(2, KVH * GRP * rows)
    grads = grads[:, : GRP * rows].reshape(KVH * GRP * rows, HD)

    there = [(m * squares + s, s * KVH + m) for m in range(KVH) for s in range(squares)]
    back = [(b, a) for a, b in there]
    p_rows = jnp.concatenate([p_lse * LOG2E, row_delta(p_grad, p_out)], axis=1).T
    p_pack = lax.ppermute(jnp.concatenate([p_query, p_grad], axis=1), "blk", there)
    p_rows = lax.ppermute(p_rows, "blk", there)

    info = jnp.stack(
        [square, square * span < lengths[0], member * p_query.shape[0], squares]
    ).astype(jnp.int32)
    spot = jnp.tile(jnp.arange(rows, dtype=jnp.int32), GRP)[None]
    fixed = (query, grads, pair)

    own, dq = own_backward(info, fixed, spot, mine)
    kv, p_pack, p_rows = together(kv, p_pack, p_rows)
    prompt_rows = (p_pack[:, :HD], p_pack[:, HD:], p_rows)
    lower, dq = lower_backward(info, fixed, kv, dq, span, pitch)
    prompt = kv.reshape(squares, pitch, 2 * HD)[:, span : span + few].reshape(blocks * part, 2 * HD)
    lower, prompt = together(lower, prompt)
    lower = lax.psum_scatter(lower, "blk", scatter_dimension=0, tiled=True, axis_index_groups=far)
    summed = (own + lower.astype(F32)).astype(BF16)

    prompt = jnp.broadcast_to(prompt[None], (rolls,) + prompt.shape)
    prompt = lax.all_to_all(prompt, "roll", 0, 0, tiled=True).reshape(-1, 2 * HD)
    prompt = prompt.reshape(rolls, blocks, part, 2 * HD).transpose(0, 2, 1, 3).reshape(-1, 2 * HD)
    prompt_terms, dq, p_dq = prompt_backward(info, fixed, prompt_rows, prompt, dq, blocks)

    prompt_terms = prompt_terms.reshape(rolls, part, blocks, 2 * HD).transpose(0, 2, 1, 3)
    prompt_terms = lax.all_to_all(prompt_terms.reshape(rolls, blocks * part, 2 * HD), "roll", 0, 0, tiled=True)
    prompt_terms = jnp.sum(prompt_terms.astype(F32), axis=0).astype(BF16)
    prompt_terms = lax.all_to_all(
        prompt_terms.reshape(squares, KVH * part, 2 * HD), "blk", 0, 0, tiled=True, axis_index_groups=far
    )
    prompt_terms = jnp.sum(prompt_terms.astype(F32), axis=0).astype(BF16)

    p_dq = lax.ppermute(p_dq, "blk", back)
    r_dq = trade(dq.reshape(KVH, GRP * rows, HD)).reshape(KVH, GRP, rows, HD)
    summed, r_dq, p_dq = together(summed, r_dq, p_dq)
    r_dq = r_dq.transpose(2, 0, 1, 3).reshape(1, rows, KVH * GRP * HD)

    summed = jnp.concatenate(
        [summed.reshape(KVH, rows, 2 * HD), prompt_terms.reshape(KVH, part, 2 * HD)], axis=1
    )
    summed = trade(summed).reshape(KVH, height, 2, HD).transpose(2, 1, 0, 3)
    summed = summed.reshape(2, height, KVH * HD)
    return (
        p_dq, summed[0, rows:], summed[1, rows:],
        r_dq, summed[0, :rows][None], summed[1, :rows][None],
    )


def solution(mesh):
    placed = (
        P("roll", "blk"),
        P(("blk", "roll"), None),
        P(("blk", "roll"), None),
        P("roll", "blk"),
        P("roll", "blk"),
        P("roll", "blk"),
        P("roll", "blk", None),
        P("roll", "blk", None),
        P("roll", "blk", None),
        P("roll", "blk", None),
        P("roll", "blk", None),
        P("roll", "blk", None),
        P("roll"),
    )
    return jax.shard_map(
        on_device,
        mesh=mesh,
        in_specs=placed,
        out_specs=(
            P("roll", "blk"),
            P(("blk", "roll"), None),
            P(("blk", "roll"), None),
            P("roll", "blk", None),
            P("roll", "blk", None),
            P("roll", "blk", None),
        ),
        check_vma=False,
    )
```

```python
import functools

import jax
import jax.numpy as jnp
from jax import lax
from jax.experimental import pallas as pl
from jax.experimental.pallas import tpu as pltpu
from jax.sharding import PartitionSpec as P

KVH = 4
HD = 128
GRP = 8
SCALE = HD ** (-0.5)
LOG2E = 1.4426950408889634
DEAD = 1e30

F32 = jnp.float32
BF16 = jnp.bfloat16
NN = (((1,), (0,)), ((), ()))
NT = (((1,), (1,)), ((), ()))
TN = (((0,), (0,)), ((), ()))


def dot(left, right, dims):
    return lax.dot_general(left, right, dims, preferred_element_type=F32)


def weigh(keys, values, query, grads, lse_row, delta_row, keep):
    scores = dot(keys, query, NT)
    dprobs = dot(values, grads, NT)
    probs = jnp.exp2(scores * (SCALE * LOG2E) - lse_row)
    if keep is not None:
        probs = jnp.where(keep, probs, 0.0)
    dscores = (probs * (dprobs - delta_row)).astype(BF16)
    return probs.astype(BF16), dscores


def terms(refs, keys, values, at, keep, acc):
    q_ref, g_ref, rows_ref = refs
    weights, dscores = weigh(
        keys, values, q_ref[at, :], g_ref[at, :], rows_ref[0:1, at], rows_ref[1:2, at], keep
    )
    acc[:, at] += dot(keys.T, dscores, NN)
    return dot(dscores, q_ref[at, :], NN), dot(weights, g_ref[at, :], NN)


def own_kernel(info, q_ref, g_ref, rows_ref, spot_ref, kv_ref, d_ref, acc):
    live = info[1]
    chunk = kv_ref.shape[0] // KVH
    group = q_ref.shape[0] // KVH
    acc[...] = jnp.zeros_like(acc)
    d_ref[...] = jnp.zeros_like(d_ref)

    @pl.when(live != 0)
    def _():
        for c in range(KVH):
            reach = (c + 1) * chunk
            place = lax.broadcasted_iota(jnp.int32, (reach, group), 0)
            dk, dv = terms(
                (q_ref, g_ref, rows_ref), kv_ref[0:reach, 0:HD], kv_ref[0:reach, HD : 2 * HD],
                slice(c * group, (c + 1) * group), place <= spot_ref[...] + c * chunk, acc,
            )
            d_ref[0:reach, 0:HD] += dk * SCALE
            d_ref[0:reach, HD : 2 * HD] += dv


def lower_kernel(info, q_ref, g_ref, rows_ref, kv_ref, dq_in, d_ref, acc, *, span, pitch):
    square, live = info[0], info[1]
    squares = kv_ref.shape[0] // pitch
    columns = q_ref.shape[0]
    group = columns // KVH
    acc[...] = dq_in[...]
    used = jnp.where(live != 0, square, 0)

    def whole(j, carry):
        source = pl.ds(pl.multiple_of(j * pitch, 16), span)
        block = pl.ds(pl.multiple_of(j * span, 16), span)
        keys, values = kv_ref[source, 0:HD], kv_ref[source, HD : 2 * HD]
        dkeys = dvalues = 0.0
        for c in range(0, columns, 2 * group):
            dk, dv = terms((q_ref, g_ref, rows_ref), keys, values, slice(c, c + 2 * group), None, acc)
            dkeys, dvalues = dkeys + dk, dvalues + dv
        d_ref[block, 0:HD] = (dkeys * SCALE).astype(BF16)
        d_ref[block, HD : 2 * HD] = dvalues.astype(BF16)
        return carry

    def empty(j, carry):
        d_ref[pl.ds(pl.multiple_of(j * span, 16), span), :] = jnp.zeros((span, 2 * HD), BF16)
        return carry

    lax.fori_loop(0, used, whole, 0)
    lax.fori_loop(used, squares, empty, 0)


def prompt_kernel(
    info, q_ref, g_ref, rows_ref, pq_ref, pg_ref, prows_ref, kv_ref, dq_in,
    d_ref, dq_ref, pdq_ref, acc, total,
    *, blocks,
):
    live, start = info[1], info[2]
    columns = q_ref.shape[0]
    group = columns // KVH
    plen = kv_ref.shape[0]
    rolls = plen // blocks
    acc[...] = dq_in[...]
    keys, values = kv_ref[:, 0:HD], kv_ref[:, HD : 2 * HD]
    shape = (plen, pq_ref.shape[0])
    index = lax.broadcasted_iota(jnp.int32, shape, 0)
    place = lax.rem(index, blocks) * rolls + lax.div(index, blocks)
    row = lax.broadcasted_iota(jnp.int32, shape, 1) + start
    weights, dscores = weigh(
        keys, values, pq_ref[...], pg_ref[...], prows_ref[0:1, :], prows_ref[1:2, :], place <= row
    )
    pdq_ref[...] = (dot(dscores, keys, TN) * SCALE).astype(BF16)
    total[:, 0:HD] = dot(dscores, pq_ref[...], NN)
    total[:, HD : 2 * HD] = dot(weights, pg_ref[...], NN)

    @pl.when(live != 0)
    def _():
        for c in range(0, columns, 2 * group):
            at = slice(c, c + 2 * group)
            dk, dv = terms((q_ref, g_ref, rows_ref), keys, values, at, None, acc)
            total[:, 0:HD] += dk
            total[:, HD : 2 * HD] += dv

    d_ref[:, 0:HD] = (total[:, 0:HD] * SCALE).astype(BF16)
    d_ref[:, HD : 2 * HD] = total[:, HD : 2 * HD].astype(BF16)
    dq_ref[...] = (acc[...].T * SCALE).astype(BF16)


def call(body, info, operands, outs, scratch, pairs, moved=4 * 1024 * 1024):
    vmem = pl.BlockSpec(memory_space=pltpu.VMEM)
    return pl.pallas_call(
        body,
        out_shape=outs,
        in_specs=[pl.BlockSpec(memory_space=pltpu.SMEM)] + [vmem] * len(operands),
        out_specs=(vmem,) * len(outs),
        scratch_shapes=scratch,
        compiler_params=pltpu.CompilerParams(vmem_limit_bytes=40 * 1024 * 1024),
        cost_estimate=pl.CostEstimate(
            flops=pairs * HD * 10, bytes_accessed=moved, transcendentals=pairs
        ),
    )(info, *operands)


def own_backward(info, fixed, spot, block):
    turned = fixed[0].shape[::-1]
    return call(
        own_kernel,
        info,
        (*fixed, spot, block),
        (jax.ShapeDtypeStruct(block.shape, F32), jax.ShapeDtypeStruct(turned, F32)),
        [],
        0,
        0,
    )


def lower_backward(info, fixed, kv, carried, span, pitch):
    query = fixed[0]
    return call(
        functools.partial(lower_kernel, span=span, pitch=pitch),
        info,
        (*fixed, kv, carried),
        (
            jax.ShapeDtypeStruct((kv.shape[0] // pitch * span, kv.shape[1]), BF16),
            jax.ShapeDtypeStruct(carried.shape, F32),
        ),
        [],
        query.shape[0] * kv.shape[0],
    )


def prompt_backward(info, fixed, prompt_rows, kv, carried, blocks):
    query = fixed[0]
    return call(
        functools.partial(prompt_kernel, blocks=blocks),
        info,
        (*fixed, *prompt_rows, kv, carried),
        (
            jax.ShapeDtypeStruct(kv.shape, BF16),
            jax.ShapeDtypeStruct(query.shape, BF16),
            jax.ShapeDtypeStruct(prompt_rows[0].shape, BF16),
        ),
        [pltpu.VMEM(carried.shape, F32), pltpu.VMEM(kv.shape, F32)],
        query.shape[0] * kv.shape[0] * 25,
    )


def row_delta(grads, outputs):
    height = grads.shape[0]
    heads = grads.shape[1] // HD
    return jnp.sum(
        grads.reshape(height, heads, HD).astype(F32) * outputs.reshape(height, heads, HD).astype(F32),
        axis=2,
    )


def three(rows):
    parts = []
    for _ in range(3):
        part = lax.reduce_precision(rows, 8, 7)
        parts.append(part.astype(BF16))
        rows = rows - part
    return jnp.concatenate(parts, axis=1)


def on_device(
    p_query, p_key, p_value, p_out, p_grad, p_lse,
    r_query, r_key, r_value, r_out, r_grad, r_lse, lengths,
):
    blocks = lax.axis_size("blk")
    rolls = lax.axis_size("roll")
    owner = lax.axis_index("blk")
    member = lax.axis_index("roll")
    squares = blocks // KVH
    square = owner // KVH
    rows = r_query.shape[1]
    span = KVH * rows
    near = [[s * KVH + m for m in range(KVH)] for s in range(squares)]

    far = [[s * KVH + m for s in range(squares)] for m in range(KVH)]
    part = p_key.shape[0]

    def trade(block):
        return lax.all_to_all(block, "blk", 0, 0, tiled=True, axis_index_groups=near)

    def together(*arrays):
        return lax.optimization_barrier(arrays)

    both = jnp.concatenate(
        [jnp.concatenate([r_key[0], r_value[0]], axis=1), jnp.concatenate([p_key, p_value], axis=1)]
    )
    height = rows + part
    both = both.reshape(height, 2, KVH, HD).transpose(2, 0, 1, 3).reshape(KVH, height, 2 * HD)
    both = trade(both)
    mine = both[:, :rows].reshape(span, 2 * HD)
    prompt = both[:, rows:].reshape(KVH * part, 2 * HD)

    position = owner * rows + jnp.arange(rows)
    alive = position < lengths[0]
    lse_rows = jnp.where(alive[:, None], r_lse[0] * LOG2E, DEAD)
    delta = row_delta(r_grad[0], r_out[0])
    pair = jnp.stack([lse_rows.T.reshape(KVH, GRP * rows), delta.T.reshape(KVH, GRP * rows)], axis=1)
    pair = three(pair.reshape(KVH, -1, HD))
    few = KVH * part
    spare = jnp.zeros((-few % 16, 2 * HD), BF16)
    pitch = span + few + spare.shape[0]
    kv = jnp.concatenate([mine, prompt, spare], axis=0)
    kv, r_query, r_grad, pair, mine = together(kv, r_query, r_grad, pair, mine)
    kv = lax.all_gather(kv, "blk", axis=0, tiled=True, axis_index_groups=far)

    def heads_first(block):
        heads = block.reshape(rows, KVH, GRP, HD).transpose(1, 2, 0, 3)
        return heads.reshape(KVH, GRP * rows, HD)

    query = trade(heads_first(r_query[0])).reshape(KVH * GRP * rows, HD)
    grads = trade(jnp.concatenate([heads_first(r_grad[0]), pair], axis=1))
    pair = grads[:, GRP * rows :].reshape(KVH, 3, 2, GRP * rows).astype(F32)
    pair = ((pair[:, 2] + pair[:, 1]) + pair[:, 0]).transpose(1, 0, 2).reshape(2, KVH * GRP * rows)
    grads = grads[:, : GRP * rows].reshape(KVH * GRP * rows, HD)

    there = [(m * squares + s, s * KVH + m) for m in range(KVH) for s in range(squares)]
    back = [(b, a) for a, b in there]
    p_rows = jnp.concatenate([p_lse * LOG2E, row_delta(p_grad, p_out)], axis=1).T
    p_pack = lax.ppermute(jnp.concatenate([p_query, p_grad], axis=1), "blk", there)
    p_rows = lax.ppermute(p_rows, "blk", there)

    info = jnp.stack(
        [square, square * span < lengths[0], member * p_query.shape[0], squares]
    ).astype(jnp.int32)
    spot = jnp.tile(jnp.arange(rows, dtype=jnp.int32), GRP)[None]
    fixed = (query, grads, pair)

    own, dq = own_backward(info, fixed, spot, mine)
    kv, p_pack, p_rows, own, dq = together(kv, p_pack, p_rows, own, dq)
    prompt_rows = (p_pack[:, :HD], p_pack[:, HD:], p_rows)
    lower, dq = lower_backward(info, fixed, kv, dq, span, pitch)
    prompt = kv.reshape(squares, pitch, 2 * HD)[:, span : span + few].reshape(blocks * part, 2 * HD)
    lower = lax.psum_scatter(lower, "blk", scatter_dimension=0, tiled=True, axis_index_groups=far)
    summed = (own + lower.astype(F32)).astype(BF16)

    prompt = jnp.broadcast_to(prompt[None], (rolls,) + prompt.shape)
    prompt = lax.all_to_all(prompt, "roll", 0, 0, tiled=True).reshape(-1, 2 * HD)
    prompt = prompt.reshape(rolls, blocks, part, 2 * HD).transpose(0, 2, 1, 3).reshape(-1, 2 * HD)
    prompt_terms, dq, p_dq = prompt_backward(info, fixed, prompt_rows, prompt, dq, blocks)

    prompt_terms = prompt_terms.reshape(rolls, part, blocks, 2 * HD).transpose(0, 2, 1, 3)
    prompt_terms = lax.all_to_all(prompt_terms.reshape(rolls, blocks * part, 2 * HD), "roll", 0, 0, tiled=True)
    prompt_terms = jnp.sum(prompt_terms.astype(F32), axis=0).astype(BF16)
    prompt_terms = lax.all_to_all(
        prompt_terms.reshape(squares, KVH * part, 2 * HD), "blk", 0, 0, tiled=True, axis_index_groups=far
    )
    prompt_terms = jnp.sum(prompt_terms.astype(F32), axis=0).astype(BF16)

    p_dq = lax.ppermute(p_dq, "blk", back)
    r_dq = trade(dq.reshape(KVH, GRP * rows, HD)).reshape(KVH, GRP, rows, HD)
    summed, r_dq, p_dq = together(summed, r_dq, p_dq)
    r_dq = r_dq.transpose(2, 0, 1, 3).reshape(1, rows, KVH * GRP * HD)

    summed = jnp.concatenate(
        [summed.reshape(KVH, rows, 2 * HD), prompt_terms.reshape(KVH, part, 2 * HD)], axis=1
    )
    summed = trade(summed).reshape(KVH, height, 2, HD).transpose(2, 1, 0, 3)
    summed = summed.reshape(2, height, KVH * HD)
    return (
        p_dq, summed[0, rows:], summed[1, rows:],
        r_dq, summed[0, :rows][None], summed[1, :rows][None],
    )


def solution(mesh):
    placed = (
        P("roll", "blk"),
        P(("blk", "roll"), None),
        P(("blk", "roll"), None),
        P("roll", "blk"),
        P("roll", "blk"),
        P("roll", "blk"),
        P("roll", "blk", None),
        P("roll", "blk", None),
        P("roll", "blk", None),
        P("roll", "blk", None),
        P("roll", "blk", None),
        P("roll", "blk", None),
        P("roll"),
    )
    return jax.shard_map(
        on_device,
        mesh=mesh,
        in_specs=placed,
        out_specs=(
            P("roll", "blk"),
            P(("blk", "roll"), None),
            P(("blk", "roll"), None),
            P("roll", "blk", None),
            P("roll", "blk", None),
            P("roll", "blk", None),
        ),
        check_vma=False,
    )
```

```python
import functools

import jax
import jax.numpy as jnp
from jax import lax
from jax.experimental import pallas as pl
from jax.experimental.pallas import tpu as pltpu
from jax.sharding import PartitionSpec as P

KVH = 4
HD = 128
GRP = 8
SCALE = HD ** (-0.5)
LOG2E = 1.4426950408889634
DEAD = 1e30

F32 = jnp.float32
BF16 = jnp.bfloat16
NN = (((1,), (0,)), ((), ()))
NT = (((1,), (1,)), ((), ()))
TN = (((0,), (0,)), ((), ()))


def dot(left, right, dims):
    return lax.dot_general(left, right, dims, preferred_element_type=F32)


def weigh(keys, values, query, grads, lse_row, delta_row, keep):
    scores = dot(keys, query, NT)
    dprobs = dot(values, grads, NT)
    probs = jnp.exp2(scores * (SCALE * LOG2E) - lse_row)
    if keep is not None:
        probs = jnp.where(keep, probs, 0.0)
    dscores = (probs * (dprobs - delta_row)).astype(BF16)
    return probs.astype(BF16), dscores


def terms(refs, keys, values, at, keep, acc):
    q_ref, g_ref, rows_ref = refs
    weights, dscores = weigh(
        keys, values, q_ref[at, :], g_ref[at, :], rows_ref[0:1, at], rows_ref[1:2, at], keep
    )
    acc[:, at] += dot(keys.T, dscores, NN)
    return dot(dscores, q_ref[at, :], NN), dot(weights, g_ref[at, :], NN)


def own_kernel(info, q_ref, g_ref, rows_ref, spot_ref, kv_ref, d_ref, acc):
    live = info[1]
    chunk = kv_ref.shape[0] // KVH
    group = q_ref.shape[0] // KVH
    acc[...] = jnp.zeros_like(acc)
    d_ref[...] = jnp.zeros_like(d_ref)

    @pl.when(live != 0)
    def _():
        for c in range(KVH):
            reach = (c + 1) * chunk
            place = lax.broadcasted_iota(jnp.int32, (reach, group), 0)
            dk, dv = terms(
                (q_ref, g_ref, rows_ref), kv_ref[0:reach, 0:HD], kv_ref[0:reach, HD : 2 * HD],
                slice(c * group, (c + 1) * group), place <= spot_ref[...] + c * chunk, acc,
            )
            d_ref[0:reach, 0:HD] += dk * SCALE
            d_ref[0:reach, HD : 2 * HD] += dv


def lower_kernel(
    info, q_ref, g_ref, rows_ref, kv_ref, d_ref, acc, taken, given, blank, in_sem, out_sem, blank_sem,
    *, span, pitch,
):
    square, live = info[0], info[1]
    squares = kv_ref.shape[0] // pitch
    columns = q_ref.shape[0]
    group = columns // KVH
    used = jnp.where(live != 0, square, 0)
    acc[...] = jnp.zeros_like(acc)
    blank[...] = jnp.zeros_like(blank)

    def place(j):
        return d_ref.at[pl.ds(pl.multiple_of(j * span, 16), span), :]

    def take(j, slot):
        source = kv_ref.at[pl.ds(pl.multiple_of(j * pitch, 16), span), :]
        return pltpu.make_async_copy(source, taken.at[slot], in_sem.at[slot])

    def give(j, slot):
        return pltpu.make_async_copy(given.at[slot], place(j), out_sem.at[slot])

    def clear(j):
        return pltpu.make_async_copy(blank, place(j), blank_sem.at[j])

    @pl.when(used > 0)
    def _():
        take(0, 0).start()

    def begin(j, carry):
        clear(j).start()
        return carry

    def whole(j, carry):
        slot = lax.rem(j, 2)

        @pl.when(j + 1 < used)
        def _():
            take(j + 1, 1 - slot).start()

        take(j, slot).wait()
        keys, values = taken[slot, :, 0:HD], taken[slot, :, HD : 2 * HD]
        dkeys = dvalues = 0.0
        for c in range(0, columns, 2 * group):
            dk, dv = terms((q_ref, g_ref, rows_ref), keys, values, slice(c, c + 2 * group), None, acc)
            dkeys, dvalues = dkeys + dk, dvalues + dv

        @pl.when(j >= 2)
        def _():
            give(j - 2, slot).wait()

        given[slot, :, 0:HD] = (dkeys * SCALE).astype(BF16)
        given[slot, :, HD : 2 * HD] = dvalues.astype(BF16)
        give(j, slot).start()
        return carry

    def end(j, carry):
        clear(j).wait()
        return carry

    lax.fori_loop(used, squares, begin, 0)
    lax.fori_loop(0, used, whole, 0)

    @pl.when(used >= 2)
    def _():
        give(used - 2, lax.rem(used, 2)).wait()

    @pl.when(used >= 1)
    def _():
        give(used - 1, lax.rem(used + 1, 2)).wait()

    lax.fori_loop(used, squares, end, 0)


def prompt_kernel(
    info, q_ref, g_ref, rows_ref, pq_ref, pg_ref, prows_ref, kv_ref, lower_dq, own_dq,
    d_ref, dq_ref, pdq_ref, acc, total,
    *, blocks,
):
    live, start = info[1], info[2]
    columns = q_ref.shape[0]
    group = columns // KVH
    plen = kv_ref.shape[0]
    rolls = plen // blocks
    acc[...] = lower_dq[...] + own_dq[...]
    keys, values = kv_ref[:, 0:HD], kv_ref[:, HD : 2 * HD]
    shape = (plen, pq_ref.shape[0])
    index = lax.broadcasted_iota(jnp.int32, shape, 0)
    place = lax.rem(index, blocks) * rolls + lax.div(index, blocks)
    row = lax.broadcasted_iota(jnp.int32, shape, 1) + start
    weights, dscores = weigh(
        keys, values, pq_ref[...], pg_ref[...], prows_ref[0:1, :], prows_ref[1:2, :], place <= row
    )
    pdq_ref[...] = (dot(dscores, keys, TN) * SCALE).astype(BF16)
    total[:, 0:HD] = dot(dscores, pq_ref[...], NN)
    total[:, HD : 2 * HD] = dot(weights, pg_ref[...], NN)

    @pl.when(live != 0)
    def _():
        for c in range(0, columns, 2 * group):
            at = slice(c, c + 2 * group)
            dk, dv = terms((q_ref, g_ref, rows_ref), keys, values, at, None, acc)
            total[:, 0:HD] += dk
            total[:, HD : 2 * HD] += dv

    d_ref[:, 0:HD] = (total[:, 0:HD] * SCALE).astype(BF16)
    d_ref[:, HD : 2 * HD] = total[:, HD : 2 * HD].astype(BF16)
    dq_ref[...] = (acc[...].T * SCALE).astype(BF16)


def call(body, info, operands, outs, scratch, pairs, moved=4 * 1024 * 1024):
    vmem = pl.BlockSpec(memory_space=pltpu.VMEM)
    return pl.pallas_call(
        body,
        out_shape=outs,
        in_specs=[pl.BlockSpec(memory_space=pltpu.SMEM)] + [vmem] * len(operands),
        out_specs=(vmem,) * len(outs),
        scratch_shapes=scratch,
        compiler_params=pltpu.CompilerParams(vmem_limit_bytes=40 * 1024 * 1024),
        cost_estimate=pl.CostEstimate(
            flops=pairs * HD * 10, bytes_accessed=moved, transcendentals=pairs
        ),
    )(info, *operands)


def own_backward(info, fixed, spot, block):
    turned = fixed[0].shape[::-1]
    return call(
        own_kernel,
        info,
        (*fixed, spot, block),
        (jax.ShapeDtypeStruct(block.shape, F32), jax.ShapeDtypeStruct(turned, F32)),
        [],
        0,
        0,
    )


def lower_backward(info, fixed, kv, span, pitch):
    query = fixed[0]
    squares = kv.shape[0] // pitch
    pairs = query.shape[0] * kv.shape[0]
    vmem = pl.BlockSpec(memory_space=pltpu.VMEM)
    whole = pl.BlockSpec(memory_space=pl.ANY)
    return pl.pallas_call(
        functools.partial(lower_kernel, span=span, pitch=pitch),
        out_shape=(
            jax.ShapeDtypeStruct((squares * span, kv.shape[1]), BF16),
            jax.ShapeDtypeStruct(query.shape[::-1], F32),
        ),
        in_specs=[pl.BlockSpec(memory_space=pltpu.SMEM), vmem, vmem, vmem, whole],
        out_specs=(whole, vmem),
        scratch_shapes=[
            pltpu.VMEM((2, span, kv.shape[1]), BF16),
            pltpu.VMEM((2, span, kv.shape[1]), BF16),
            pltpu.VMEM((span, kv.shape[1]), BF16),
            pltpu.SemaphoreType.DMA((2,)),
            pltpu.SemaphoreType.DMA((2,)),
            pltpu.SemaphoreType.DMA((squares,)),
        ],
        compiler_params=pltpu.CompilerParams(vmem_limit_bytes=40 * 1024 * 1024),
        cost_estimate=pl.CostEstimate(
            flops=pairs * HD * 10, bytes_accessed=4 * 1024 * 1024, transcendentals=pairs
        ),
    )(info, *fixed, kv)


def prompt_backward(info, fixed, prompt_rows, kv, carried, blocks):
    query = fixed[0]
    return call(
        functools.partial(prompt_kernel, blocks=blocks),
        info,
        (*fixed, *prompt_rows, kv, *carried),
        (
            jax.ShapeDtypeStruct(kv.shape, BF16),
            jax.ShapeDtypeStruct(query.shape, BF16),
            jax.ShapeDtypeStruct(prompt_rows[0].shape, BF16),
        ),
        [pltpu.VMEM(carried[0].shape, F32), pltpu.VMEM(kv.shape, F32)],
        query.shape[0] * kv.shape[0],
    )


def row_delta(grads, outputs):
    height = grads.shape[0]
    heads = grads.shape[1] // HD
    return jnp.sum(
        grads.reshape(height, heads, HD).astype(F32) * outputs.reshape(height, heads, HD).astype(F32),
        axis=2,
    )


def three(rows):
    parts = []
    for _ in range(3):
        part = lax.reduce_precision(rows, 8, 7)
        parts.append(part.astype(BF16))
        rows = rows - part
    return jnp.concatenate(parts, axis=1)


def on_device(
    p_query, p_key, p_value, p_out, p_grad, p_lse,
    r_query, r_key, r_value, r_out, r_grad, r_lse, lengths,
):
    blocks = lax.axis_size("blk")
    rolls = lax.axis_size("roll")
    owner = lax.axis_index("blk")
    member = lax.axis_index("roll")
    squares = blocks // KVH
    square = owner // KVH
    rows = r_query.shape[1]
    span = KVH * rows
    near = [[s * KVH + m for m in range(KVH)] for s in range(squares)]

    far = [[s * KVH + m for s in range(squares)] for m in range(KVH)]
    part = p_key.shape[0]

    def trade(block):
        return lax.all_to_all(block, "blk", 0, 0, tiled=True, axis_index_groups=near)

    def together(*arrays):
        return lax.optimization_barrier(arrays)

    both = jnp.concatenate(
        [jnp.concatenate([r_key[0], r_value[0]], axis=1), jnp.concatenate([p_key, p_value], axis=1)]
    )
    height = rows + part
    both = both.reshape(height, 2, KVH, HD).transpose(2, 0, 1, 3).reshape(KVH, height, 2 * HD)
    both = trade(both)
    mine = both[:, :rows].reshape(span, 2 * HD)
    prompt = both[:, rows:].reshape(KVH * part, 2 * HD)

    position = owner * rows + jnp.arange(rows)
    alive = position < lengths[0]
    lse_rows = jnp.where(alive[:, None], r_lse[0] * LOG2E, DEAD)
    delta = row_delta(r_grad[0], r_out[0])
    pair = jnp.stack([lse_rows.T.reshape(KVH, GRP * rows), delta.T.reshape(KVH, GRP * rows)], axis=1)
    pair = three(pair.reshape(KVH, -1, HD))
    few = KVH * part
    spare = jnp.zeros((-few % 16, 2 * HD), BF16)
    pitch = span + few + spare.shape[0]
    kv = jnp.concatenate([mine, prompt, spare], axis=0)
    kv, r_query, r_grad, pair, mine = together(kv, r_query, r_grad, pair, mine)
    kv = lax.all_gather(kv, "blk", axis=0, tiled=True, axis_index_groups=far)

    def heads_first(block):
        heads = block.reshape(rows, KVH, GRP, HD).transpose(1, 2, 0, 3)
        return heads.reshape(KVH, GRP * rows, HD)

    query = trade(heads_first(r_query[0])).reshape(KVH * GRP * rows, HD)
    grads = trade(jnp.concatenate([heads_first(r_grad[0]), pair], axis=1))
    pair = grads[:, GRP * rows :].reshape(KVH, 3, 2, GRP * rows).astype(F32)
    pair = ((pair[:, 2] + pair[:, 1]) + pair[:, 0]).transpose(1, 0, 2).reshape(2, KVH * GRP * rows)
    grads = grads[:, : GRP * rows].reshape(KVH * GRP * rows, HD)

    there = [(m * squares + s, s * KVH + m) for m in range(KVH) for s in range(squares)]
    back = [(b, a) for a, b in there]
    p_rows = jnp.concatenate([p_lse * LOG2E, row_delta(p_grad, p_out)], axis=1).T
    p_pack = lax.ppermute(jnp.concatenate([p_query, p_grad], axis=1), "blk", there)
    p_rows = lax.ppermute(p_rows, "blk", there)

    info = jnp.stack(
        [square, square * span < lengths[0], member * p_query.shape[0], squares]
    ).astype(jnp.int32)
    spot = jnp.tile(jnp.arange(rows, dtype=jnp.int32), GRP)[None]
    fixed = (query, grads, pair)

    own, own_dq = own_backward(info, fixed, spot, mine)
    kv, p_pack, p_rows, own, own_dq = together(kv, p_pack, p_rows, own, own_dq)
    prompt_rows = (p_pack[:, :HD], p_pack[:, HD:], p_rows)
    lower, lower_dq = lower_backward(info, fixed, kv, span, pitch)
    prompt = kv.reshape(squares, pitch, 2 * HD)[:, span : span + few].reshape(blocks * part, 2 * HD)
    lower, prompt = together(lower, prompt)
    lower = lax.psum_scatter(lower, "blk", scatter_dimension=0, tiled=True, axis_index_groups=far)
    summed = (own + lower.astype(F32)).astype(BF16)

    prompt = jnp.broadcast_to(prompt[None], (rolls,) + prompt.shape)
    prompt = lax.all_to_all(prompt, "roll", 0, 0, tiled=True).reshape(-1, 2 * HD)
    prompt = prompt.reshape(rolls, blocks, part, 2 * HD).transpose(0, 2, 1, 3).reshape(-1, 2 * HD)
    prompt_terms, dq, p_dq = prompt_backward(
        info, fixed, prompt_rows, prompt, (lower_dq, own_dq), blocks
    )

    place = owner % KVH
    dq = dq.reshape(KVH, GRP * rows, HD)
    r_dq = jnp.zeros_like(dq)
    pieces = []
    for distance in range(KVH):
        partner = place ^ distance
        piece = lax.dynamic_index_in_dim(dq, partner, 0, keepdims=True)
        if distance:
            piece = lax.ppermute(piece, "blk", [(i, i ^ distance) for i in range(blocks)])
        pieces.append(piece)

    prompt_terms = prompt_terms.reshape(rolls, part, blocks, 2 * HD).transpose(0, 2, 1, 3)
    prompt_terms = lax.all_to_all(prompt_terms.reshape(rolls, blocks * part, 2 * HD), "roll", 0, 0, tiled=True)
    prompt_terms = jnp.sum(prompt_terms.astype(F32), axis=0).astype(BF16)
    prompt_terms, *pieces = together(prompt_terms, *pieces)
    for distance, piece in enumerate(pieces):
        r_dq = lax.dynamic_update_slice_in_dim(r_dq, piece, place ^ distance, 0)
    r_dq = r_dq.reshape(KVH, GRP, rows, HD)
    prompt_terms = lax.all_to_all(
        prompt_terms.reshape(squares, KVH * part, 2 * HD), "blk", 0, 0, tiled=True, axis_index_groups=far
    )
    prompt_terms = jnp.sum(prompt_terms.astype(F32), axis=0).astype(BF16)

    p_dq = lax.ppermute(p_dq, "blk", back)
    summed, r_dq, p_dq = together(summed, r_dq, p_dq)
    r_dq = r_dq.transpose(2, 0, 1, 3).reshape(1, rows, KVH * GRP * HD)

    summed = jnp.concatenate(
        [summed.reshape(KVH, rows, 2 * HD), prompt_terms.reshape(KVH, part, 2 * HD)], axis=1
    )
    summed = trade(summed).reshape(KVH, height, 2, HD).transpose(2, 1, 0, 3)
    summed = summed.reshape(2, height, KVH * HD)
    return (
        p_dq, summed[0, rows:], summed[1, rows:],
        r_dq, summed[0, :rows][None], summed[1, :rows][None],
    )


def solution(mesh):
    placed = (
        P("roll", "blk"),
        P(("blk", "roll"), None),
        P(("blk", "roll"), None),
        P("roll", "blk"),
        P("roll", "blk"),
        P("roll", "blk"),
        P("roll", "blk", None),
        P("roll", "blk", None),
        P("roll", "blk", None),
        P("roll", "blk", None),
        P("roll", "blk", None),
        P("roll", "blk", None),
        P("roll"),
    )
    return jax.shard_map(
        on_device,
        mesh=mesh,
        in_specs=placed,
        out_specs=(
            P("roll", "blk"),
            P(("blk", "roll"), None),
            P(("blk", "roll"), None),
            P("roll", "blk", None),
            P("roll", "blk", None),
            P("roll", "blk", None),
        ),
        check_vma=False,
    )
```
